1024 devices in a mesh: row: 128 (over z, x), col: 4 (over y), rep: 2 (over core).
Axes of the slice: x: 4, y: 4, z: 32, core: 2. Of those that a mesh axis runs over, the one named last changes fastest.
Arguments:
- output_grad: bfloat16 [131072, 256], P(('row', 'col', 'rep')), may hold values from -6 to 6
- pooled: bfloat16 [131072, 64], P(('row', 'col', 'rep')), may hold values from -6 to 6
- bag_owners: int32 [131072, 4], P(('row', 'col', 'rep')), may hold values from 0 to 127, all different within a row; in each aligned block of 128 rows (0 to 127, 128 to 255, ...) at most 6 rows name the same one
- bag_rows: int32 [131072, 4], P(('row', 'col', 'rep')), may hold values from 0 to 4095
- bag_weights: float32 [131072, 4], P(('row', 'col', 'rep')), may hold values from 0.5 to 2
- embed_table: float32 [524288, 64], P('row'), may hold values from -6 to 6
- table_state: float32 [524288], P('row'), may hold values from 0.5 to 8
- projection: float32 [64, 256], replicated, may hold values from -0.75 to 0.75
- projection_state: float32 [64, 256], replicated, may hold values from 32768 to 2097152
Outputs:
- new_table: float32 [524288, 64], P('row')
- new_table_state: float32 [524288], P('row')
- new_projection: float32 [64, 256], replicated
- new_projection_state: float32 [64, 256], replicated
The draws below stay inside these ranges and needn't reach their ends.
Inputs may be any that keep to these rules, and one draw needn't show every extreme that they name: `bag_owners`: the 4 entries of a sample name different owners; among the 128 samples of one device no owner is named by more than 6 entries, a bound that some block reaches.
All inputs are finite; a program needn't handle non-finite values.
Results may differ from the reference program's by a relative error of at most 0.0013.
Values may be sent and summed in bfloat16 or wider, within the bound.
No kernel may reach another device: no remote copies, remote signals or barrier semaphores. Data moves between devices by JAX's collectives and lax.ppermute only.
A program may use at most 32 MiB of HBM per device.

```python
import math
import jax
import jax.numpy as jnp
import numpy as np
from jax import lax

DN = 64
PROJ = 256
BAG = 4
S_DEV = 128
V_DEV = 4096
CAP = 6
SAMPLES = 131072
VOCAB = 524288
N_ROW = 128


def with_ends(values, stream_key, least, top_value):
    longest = values.shape.index(max(values.shape))
    spots = []
    for shift in (0, 1):
        where = [jax.random.randint(jax.random.fold_in(stream_key, axis), (), 0, length) for axis, length in enumerate(values.shape)]
        where[longest] = (where[longest] + shift) % values.shape[longest]
        spots.append(tuple(where))
    return values.at[spots[0]].set(least).at[spots[1]].set(top_value)


def block_levels(stream_key, extent, pieces, smallest, high):
    loudness = 1.0
    for axis_at, shards_of in pieces:
        steps = jax.random.uniform(jax.random.fold_in(jax.random.fold_in(stream_key, 6), axis_at), (shards_of,), jnp.float32, smallest / len(pieces), high / len(pieces))
        loudness = loudness * jnp.repeat(jnp.exp(steps), extent[axis_at] // shards_of).reshape((-1,) + (1,) * (len(extent) - 1 - axis_at))
    return loudness


def routed_block(own_key, own, number, rows, amount, top, bound, skew):
    order = jax.random.permutation(own_key, amount)
    heavy_load, ordinary = portions_of(amount, rows * top, bound, skew, True), portions_of(amount, rows * top, bound, skew, False)
    places = jnp.arange(amount)

    def named(tallies, rotation):
        used = int((tallies > 0).sum())
        fixed = max(1, used // 4)
        moved = fixed + (places - fixed + rotation * (used - fixed)) % max(1, amount - fixed)
        return jnp.zeros((amount,), jnp.int32).at[order[jnp.where(places < fixed, places, moved)]].set(jnp.asarray(tallies, jnp.int32))

    tallies = jnp.where(number % 4 == 0, named(heavy_load, number // 4), named(ordinary, number - number // 4 - 1))
    mixed = jax.random.permutation(jax.random.fold_in(own, 3), amount)
    donor, sink = mixed[0:amount // 2 * 2:2], mixed[1:amount // 2 * 2:2]
    room = jnp.minimum(tallies[donor] - 1, bound - tallies[sink]) // 2
    room = jnp.where((donor == order[0]) | (sink == order[0]) | (tallies[sink] == 0), 0, jnp.maximum(room, 0))
    moved = jax.random.randint(jax.random.fold_in(own, 4), (amount // 2,), 0, 1 << 20) % (room + 1)
    tallies = tallies.at[donor].add(-moved).at[sink].add(moved)
    labels = jnp.searchsorted(jnp.cumsum(tallies), jnp.arange(rows * top), side="right").astype(jnp.int32)
    listing = labels.reshape(top, rows).T
    listing = listing[jax.random.permutation(jax.random.fold_in(own, 1), rows)]
    rotation = jax.random.randint(jax.random.fold_in(own, 2), (rows, 1), 0, top)
    return jnp.take_along_axis(listing, (jnp.arange(top)[None, :] + rotation) % top, axis=1)


def portions_of(amount, total, bound, skew, full):
    portions = [(1 << 20) // math.isqrt(standing ** skew) + 1 for standing in range(1, amount + 1)]
    largest = bound if full else min(bound, max(-(-total // amount), total * portions[0] // sum(portions)))
    least = 1 if total - largest >= amount - 1 else 0
    counts, spare = [largest] + [least] * (amount - 1), total - largest - least * (amount - 1)
    while spare > 0:
        free = [i for i in range(1, amount) if counts[i] < largest] or [i for i in range(1, amount) if counts[i] < bound]
        mass, left = sum([portions[i] for i in free]), spare
        for i in free:
            extra = min(bound - counts[i], max(1, left * portions[i] // mass), spare)
            counts[i] = counts[i] + extra
            spare = spare - extra
    return np.array(counts)


def scatter_about(rng, dims, width, most, pieces=(), dtype=jnp.bfloat16):
    array = width * jax.random.normal(rng, dims, jnp.float32)
    if pieces:
        array = array * block_levels(rng, dims, pieces, -0.22, 0.18)
    return jnp.clip(array, -most, most).astype(dtype)


def setup_inputs(seed: int = 0) -> dict:
    splits = jax.random.split(jax.random.key(seed), 10)
    output_grad = scatter_about(splits[0], (SAMPLES, PROJ), 1.0, 6.0, ((0, 1024),))
    pooled = scatter_about(splits[1], (SAMPLES, DN), 1.0, 6.0, ((0, 1024),))
    bag_owners_keys = jax.random.split(jax.random.fold_in(splits[2], 1), SAMPLES // S_DEV)
    bag_owners_turns = jax.random.permutation(jax.random.fold_in(splits[2], 3), SAMPLES // S_DEV)
    bag_owners = jax.vmap(lambda own, number: routed_block(jax.random.fold_in(splits[2], 2), own, number, S_DEV, N_ROW, BAG, CAP, 2))(bag_owners_keys, bag_owners_turns).reshape((SAMPLES, BAG))
    bag_rows = with_ends(jax.random.randint(splits[3], (SAMPLES, BAG), 0, V_DEV), jax.random.fold_in(splits[3], 1), 0, V_DEV - 1).astype(jnp.int32)
    bag_weights = jnp.clip(0.5 + 1.5 * jax.random.uniform(splits[4], (SAMPLES, BAG), jnp.float32) ** block_levels(splits[4], (SAMPLES, BAG), ((0, 1024),), -0.2, 0.2), 0.5, 2.0)
    embed_table = scatter_about(splits[5], (VOCAB, DN), 1.0, 6.0, ((0, 128),), jnp.float32)
    table_state = jnp.clip(jnp.exp(math.log(8.0) - 2.7725887 * jax.random.uniform(splits[6], (VOCAB,), jnp.float32) ** block_levels(splits[6], (VOCAB,), ((0, 128),), -0.2, 0.2)), 0.5, 8.0)
    projection = scatter_about(splits[7], (DN, PROJ), DN ** -0.5, 0.75, (), jnp.float32)
    projection_state = jnp.clip(jnp.exp(jax.random.uniform(splits[8], (DN, PROJ), jnp.float32, math.log(32768.0), math.log(2097152))), 32768.0, 2097152)
    return dict(output_grad=output_grad, pooled=pooled, bag_owners=bag_owners, bag_rows=bag_rows, bag_weights=bag_weights, embed_table=embed_table, table_state=table_state, projection=projection, projection_state=projection_state)


learn_rate = 0.5
epsilon = 1e-06

def reference(output_grad, pooled, bag_owners, bag_rows, bag_weights, embed_table, table_state, projection, projection_state):
    projection_low = projection.astype(jnp.bfloat16)
    pool_grad = jnp.dot(output_grad, projection_low.T, preferred_element_type=jnp.float32)
    grad_rows = (bag_weights[:, :, None] * pool_grad[:, None, :]).astype(jnp.bfloat16)
    global_index = (bag_owners * V_DEV + bag_rows).reshape(-1).astype(jnp.int32)
    flat_rows = grad_rows.reshape(-1, DN).astype(jnp.float32)
    dense_grad = jnp.zeros((V_DEV * N_ROW, DN), jnp.float32).at[global_index].add(flat_rows)
    new_table_state = table_state + lax.optimization_barrier(jnp.mean(dense_grad * dense_grad, axis=1))
    new_table = embed_table - learn_rate * dense_grad / (jnp.sqrt(new_table_state)[:, None] + epsilon)
    weight_grad = jnp.dot(pooled.T, output_grad, preferred_element_type=jnp.float32)
    new_projection_state = projection_state + weight_grad * weight_grad
    new_projection = projection - learn_rate * weight_grad / (jnp.sqrt(new_projection_state) + epsilon)
    return (new_table, new_table_state, new_projection, new_projection_state)
```

```python
import functools

import jax
import jax.numpy as jnp
from jax import lax
from jax.experimental import pallas as pl
from jax.experimental.pallas import tpu as pltpu
from jax.sharding import Mesh
from jax.sharding import PartitionSpec as P

learn_rate = 0.5
epsilon = 1e-06

X = 4
CAP = 6
QUAD = 4
PLANE = ("x", "col", "rep")
LOW = jnp.bfloat16
FULL = jnp.float32

NT = (((1,), (1,)), ((), ()))
TN = (((0,), (0,)), ((), ()))


def dot(a, b, dims):
    return lax.dot_general(a, b, dims, preferred_element_type=FULL)


def iota(shape, dim):
    return lax.broadcasted_iota(jnp.int32, shape, dim)


def halves(value):
    high = value.astype(LOW).astype(FULL)
    return jnp.concatenate([high, value - high], axis=0)


def route_kernel(*refs):
    ins, outs, held, sems = refs[:6], refs[6:8], refs[8:14], refs[14]
    copies = [
        pltpu.make_async_copy(ins[n], held[n], sems.at[n]) for n in range(len(ins))
    ]
    for copy in copies:
        copy.start()
    for copy in copies:
        copy.wait()
    output_grad, pooled_t, projection, owners, rows, weights = held
    shares, out = outs

    grad = jnp.dot(pooled_t[...], output_grad[...], preferred_element_type=FULL)
    for i in range(shares.shape[0]):
        r, c = 4 * (i // 2), 128 * (i % 2)
        shares[i] = grad[r : r + 4, c : c + 128]

    bag, samples = owners.shape
    entries = bag * samples
    width = projection.shape[0]
    slabs, slab_rows, lanes = out.shape
    owner_count = slabs * X

    def flat(ref):
        return jnp.concatenate([ref[k : k + 1, :] for k in range(bag)], axis=1)

    pool_grad = dot(projection[...].astype(LOW), output_grad[...], NT)
    grads = jnp.concatenate(
        [(pool_grad * weights[k : k + 1, :]).astype(LOW) for k in range(bag)], axis=1
    )
    owner, row = flat(owners), flat(rows)
    hits = jnp.where(iota((owner_count, entries), 0) == owner, 1.0, 0.0)
    before = jnp.where(iota((entries, entries), 0) < iota((entries, entries), 1), 1.0, 0.0)
    earlier = jnp.dot(hits.astype(LOW), before.astype(LOW), preferred_element_type=FULL)
    rank = jnp.sum(hits * earlier, axis=0, keepdims=True).astype(jnp.int32)
    odd = rank & 1
    base = owner * QUAD
    pair_at = base + (rank >> 1)
    place = iota((slabs * slab_rows, entries), 0)

    def chosen(at):
        return jnp.where(place == at, 1.0, 0.0).astype(LOW)

    picks = jnp.concatenate(
        [
            chosen(jnp.where(odd == 0, pair_at, -1)),
            chosen(jnp.where(odd == 1, pair_at, -1)),
            chosen(base + (QUAD - 1)),
        ],
        axis=1,
    )
    blank = jnp.zeros((width, entries), LOW)
    lane = iota((lanes, entries), 0)
    numbers = jnp.where(lane == 2 * rank, row >> 8, 0) + jnp.where(
        lane == 2 * rank + 1, row & 255, 0
    )
    values = jnp.concatenate(
        [
            jnp.concatenate([grads, blank], axis=0),
            jnp.concatenate([blank, grads], axis=0),
            numbers.astype(FULL).astype(LOW),
        ],
        axis=1,
    )
    sent = dot(picks, values, NT).astype(LOW)
    for i in range(slabs):
        out[(i + slabs // 2) % slabs] = sent[i * slab_rows : (i + 1) * slab_rows, :]


def join_kernel(sent, shares, out):
    slabs, slab_rows, _ = sent.shape
    share = halves(jnp.sum(shares[...], axis=0)).astype(LOW)
    for i in range(slabs):
        out[i, 0:slab_rows, :] = sent[i]
        out[i, slab_rows:, :] = share


def regroup_kernel(got, out):
    slabs, _, lanes = got.shape
    width = lanes // 2
    slab_rows = X * QUAD
    copies = out.shape[0] // X
    count = slabs * slab_rows
    flat = got[:, 0:slab_rows, :].reshape(count, lanes)

    def source(lane, pairs, first):
        block = 2 * pairs * slabs
        within = lane % block
        pair = (within // slabs) % pairs + first
        return (within % slabs) * slab_rows + (lane // block) * QUAD, pair, within // (
            slabs * pairs
        )

    def turned(pairs, first):
        size = X * 2 * pairs * slabs
        lane = iota((count, size), 1)
        row = iota((count, size), 0)
        slab, pair, odd = source(lane, pairs, first)
        at = slab + pair
        even_move = jnp.where((row == at) & (odd == 0), 1.0, 0.0).astype(LOW)
        odd_move = jnp.where((row == at) & (odd == 1), 1.0, 0.0).astype(LOW)
        move = jnp.where(row == slab + (QUAD - 1), 1.0, 0.0).astype(LOW)
        data = dot(flat[:, 0:width], even_move, TN) + dot(flat[:, width:], odd_move, TN)
        spread = dot(flat, move, TN)[0:16, :]
        down = iota((16, size), 0)
        _, pair, odd = source(iota((16, size), 1), pairs, first)
        slot = 2 * (2 * pair + odd)
        high = jnp.sum(jnp.where(down == slot, spread, 0.0), axis=0, keepdims=True)
        low = jnp.sum(jnp.where(down == slot + 1, spread, 0.0), axis=0, keepdims=True)
        return data.astype(LOW), high, low

    many, many_high, many_low = turned(2, 0)
    few, few_high, few_low = turned(1, 2)
    total = jnp.sum(got[:, slab_rows:, :].astype(FULL), axis=0)
    tail = halves(total[0:4, :] + total[4:8, :])
    blank = jnp.zeros((5, lanes), FULL)
    for x in range(X):
        here = slice(x * lanes, (x + 1) * lanes)
        half = slice(x * width, (x + 1) * width)
        rest = jnp.concatenate([few[0 : width // 2, half], few[width // 2 :, half]], axis=1)
        last = jnp.concatenate(
            [
                many_high[:, here],
                many_low[:, here],
                jnp.concatenate([few_high[:, half], few_low[:, half]], axis=1),
                blank,
                tail,
            ],
            axis=0,
        ).astype(LOW)
        for j in range(copies):
            out[x * copies + j, 0:width, :] = many[:, here]
            out[x * copies + j, width : width + width // 2, :] = rest
            out[x * copies + j, width + width // 2 :, :] = last


def update_kernel(
    got,
    table,
    state,
    projection,
    projection_state,
    new_table,
    new_state,
    new_projection,
    new_projection_state,
    spread,
    marks,
    total,
    grad,
    *,
    group,
):
    reps, peers, rows, lanes = got.shape
    width, table_rows = table.shape
    half = width // 2
    low_count = 256
    high_count = table_rows // low_count
    marked = iota((low_count, lanes), 0).astype(FULL).astype(LOW)

    def put(at, entry, high, low):
        cols = slice(at, at + lanes)
        high = jnp.broadcast_to(high, (width, lanes)).astype(LOW)
        low = jnp.broadcast_to(low, (low_count, lanes)).astype(LOW)
        for h in range(high_count):
            spread[h * width : (h + 1) * width, cols] = jnp.where(
                high == h, entry, jnp.zeros_like(entry)
            )
        marks[:, cols] = jnp.where(low == marked, 1.0, 0.0).astype(LOW)

    def beside(a, b):
        first = jnp.concatenate([a[:, 0:width], b[:, 0:width]], axis=1)
        second = jnp.concatenate([a[:, width:], b[:, width:]], axis=1)
        return first, second

    for first in range(0, peers, group):
        at = 0
        for n in range(first, first + group):
            pair = [got.at[r, n] for r in range(reps)]
            numbers = [block[width + half : rows, :].astype(FULL) for block in pair]
            for block, number in zip(pair, numbers, strict=True):
                put(at, block[0:width, :], number[0:1, :], number[1:2, :])
                at += lanes
            top, bottom = beside(*[block[width : width + half, :] for block in pair])
            high, low = beside(*[number[2:3, :] for number in numbers])
            put(at, jnp.concatenate([top, bottom], axis=0), high, low)
            at += lanes
        part = dot(spread[...], marks[...], NT)
        if first == 0:
            total[...] = part
        else:
            total[...] += part

    for h in range(high_count):
        cols = slice(h * low_count, (h + 1) * low_count)
        dense = total[h * width : (h + 1) * width, :]
        fresh = state[:, cols] + jnp.sum(dense * dense, axis=0, keepdims=True) * (1.0 / width)
        new_state[:, cols] = fresh
        new_table[:, cols] = table[:, cols] - learn_rate * dense / (jnp.sqrt(fresh) + epsilon)

    for i in range(reps * peers):
        r, c = 4 * (i // 2), 128 * (i % 2)
        tail = got[i % reps, i // reps, width + half : rows, :].astype(FULL)
        grad[r : r + 4, c : c + 128] = tail[8:12, :] + tail[12:16, :]
    whole = grad[...]
    fresh = projection_state[...] + whole * whole
    new_projection_state[...] = fresh
    new_projection[...] = projection[...] - learn_rate * whole / (jnp.sqrt(fresh) + epsilon)


def call(kernel, outs, *args, scratch=(), where=pltpu.VMEM):
    spec = pl.BlockSpec(memory_space=pltpu.VMEM)
    return pl.pallas_call(
        kernel,
        out_shape=outs,
        in_specs=[pl.BlockSpec(memory_space=where)] * len(args),
        out_specs=jax.tree.map(lambda _: spec, outs),
        scratch_shapes=list(scratch),
        compiler_params=pltpu.CompilerParams(vmem_limit_bytes=40 * 2**20),
    )(*args)


def shards(
    output_grad,
    pooled,
    bag_owners,
    bag_rows,
    bag_weights,
    embed_table,
    table_state,
    projection,
    projection_state,
):
    depth = lax.axis_size("z")
    peers = lax.axis_size(PLANE)
    reps = lax.axis_size("rep")
    table_rows, width = embed_table.shape
    lanes = 2 * width

    with jax.named_scope("route"):
        inputs = (
            output_grad,
            pooled.T,
            projection,
            bag_owners.T,
            bag_rows.T,
            bag_weights.T,
        )
        shares, sent = call(
            route_kernel,
            (
                jax.ShapeDtypeStruct((peers, 4, 128), FULL),
                jax.ShapeDtypeStruct((depth, X * QUAD, lanes), LOW),
            ),
            *inputs,
            scratch=[pltpu.VMEM(a.shape, a.dtype) for a in inputs]
            + [pltpu.SemaphoreType.DMA((len(inputs),))],
            where=pltpu.HBM,
        )
    with jax.named_scope("weight_plane"):
        shares = lax.all_to_all(shares, PLANE, 0, 0, tiled=True)
    with jax.named_scope("join"):
        sent = call(
            join_kernel,
            jax.ShapeDtypeStruct((depth, X * QUAD + 8, lanes), LOW),
            sent,
            shares,
        )
    ring = [[(i + depth // 2) % depth for i in range(depth)]]
    with jax.named_scope("along_z"):
        got = lax.all_to_all(sent, "z", 0, 0, axis_index_groups=ring, tiled=True)
    with jax.named_scope("regroup"):
        sent = call(
            regroup_kernel,
            jax.ShapeDtypeStruct((peers // reps, width + width // 2 + 16, lanes), LOW),
            got,
        )
    with jax.named_scope("in_plane"):
        got = lax.all_to_all(sent, ("x", "col"), 0, 0, tiled=True)
    with jax.named_scope("on_chip"):
        got = lax.all_gather(got, "rep")
    with jax.named_scope("update"):
        group = 4
        columns = group * (reps + 1) * lanes
        new_table, new_state, new_projection, new_projection_state = call(
            functools.partial(update_kernel, group=group),
            (
                jax.ShapeDtypeStruct((width, table_rows), FULL),
                jax.ShapeDtypeStruct((1, table_rows), FULL),
                jax.ShapeDtypeStruct(projection.shape, FULL),
                jax.ShapeDtypeStruct(projection.shape, FULL),
            ),
            got,
            embed_table.T,
            table_state.reshape(1, table_rows),
            projection,
            projection_state,
            scratch=(
                pltpu.VMEM((table_rows // 256 * width, columns), LOW),
                pltpu.VMEM((256, columns), LOW),
                pltpu.VMEM((table_rows // 256 * width, 256), FULL),
                pltpu.VMEM(projection.shape, FULL),
            ),
        )
    return (
        new_table.T,
        new_state.reshape(table_rows),
        new_projection,
        new_projection_state,
    )


def solution(mesh):
    sizes = mesh.shape
    fine = Mesh(
        mesh.devices.reshape(sizes["row"] // X, X, sizes["col"], sizes["rep"]),
        ("z", "x", "col", "rep"),
    )
    split = P(("z", "x", "col", "rep"), None)
    owned = ("z", "x")
    return jax.shard_map(
        shards,
        mesh=fine,
        in_specs=(split,) * 5 + (P(owned, None), P(owned), P(), P()),
        out_specs=(P(owned, None), P(owned), P(), P()),
        check_vma=False,
    )
```

```python
import jax
import jax.numpy as jnp
from jax import lax
from jax.experimental import pallas as pl
from jax.experimental.pallas import tpu as pltpu
from jax.sharding import Mesh
from jax.sharding import PartitionSpec as P

learn_rate = 0.5
epsilon = 1e-06

X = 4
CAP = 6
STEP = 16
QUAD = 4
PLANE = ("x", "col", "rep")
LOW = jnp.bfloat16
FULL = jnp.float32

NT = (((1,), (1,)), ((), ()))
TN = (((0,), (0,)), ((), ()))


def dot(a, b, dims):
    return lax.dot_general(a, b, dims, preferred_element_type=FULL)


def iota(shape, dim):
    return lax.broadcasted_iota(jnp.int32, shape, dim)


def halves(value):
    high = value.astype(LOW).astype(FULL)
    return jnp.concatenate([high, value - high], axis=0)


def route_kernel(*refs):
    ins, outs, held, sems = refs[:6], refs[6:8], refs[8:14], refs[14]
    copies = [
        pltpu.make_async_copy(ins[n], held[n], sems.at[n]) for n in range(len(ins))
    ]
    for copy in copies:
        copy.start()
    for copy in copies:
        copy.wait()
    output_grad, pooled_t, projection, owners, rows, weights = held
    shares, out = outs

    grad = jnp.dot(pooled_t[...], output_grad[...], preferred_element_type=FULL)
    for i in range(shares.shape[0]):
        r, c = 4 * (i // 2), 128 * (i % 2)
        shares[i] = grad[r : r + 4, c : c + 128]

    bag, samples = owners.shape
    entries = bag * samples
    width = projection.shape[0]
    slabs, slab_rows, lanes = out.shape
    owner_count = slabs * X

    def flat(ref):
        return jnp.concatenate([ref[k : k + 1, :] for k in range(bag)], axis=1)

    pool_grad = dot(projection[...].astype(LOW), output_grad[...], NT)
    grads = jnp.concatenate(
        [(pool_grad * weights[k : k + 1, :]).astype(LOW) for k in range(bag)], axis=1
    )
    owner, row = flat(owners), flat(rows)
    hits = jnp.where(iota((owner_count, entries), 0) == owner, 1.0, 0.0)
    before = jnp.where(iota((entries, entries), 0) < iota((entries, entries), 1), 1.0, 0.0)
    earlier = jnp.dot(hits.astype(LOW), before.astype(LOW), preferred_element_type=FULL)
    rank = jnp.sum(hits * earlier, axis=0, keepdims=True).astype(jnp.int32)
    odd = rank & 1
    base = owner * QUAD
    pair_at = base + (rank >> 1)
    place = iota((slabs * slab_rows, entries), 0)

    def chosen(at):
        return jnp.where(place == at, 1.0, 0.0).astype(LOW)

    picks = jnp.concatenate(
        [
            chosen(jnp.where(odd == 0, pair_at, -1)),
            chosen(jnp.where(odd == 1, pair_at, -1)),
            chosen(base + (QUAD - 1)),
        ],
        axis=1,
    )
    blank = jnp.zeros((width, entries), LOW)
    lane = iota((lanes, entries), 0)
    numbers = jnp.where(lane == 2 * rank, row >> 8, 0) + jnp.where(
        lane == 2 * rank + 1, row & 255, 0
    )
    values = jnp.concatenate(
        [
            jnp.concatenate([grads, blank], axis=0),
            jnp.concatenate([blank, grads], axis=0),
            numbers.astype(FULL).astype(LOW),
        ],
        axis=1,
    )
    sent = dot(picks, values, NT).astype(LOW)
    for i in range(slabs):
        out[(i + slabs // 2) % slabs] = sent[i * slab_rows : (i + 1) * slab_rows, :]


def join_kernel(sent, shares, out):
    slabs, slab_rows, _ = sent.shape
    share = halves(jnp.sum(shares[...], axis=0)).astype(LOW)
    for i in range(slabs):
        out[i, 0:slab_rows, :] = sent[i]
        out[i, slab_rows:, :] = share


def regroup_kernel(got, out):
    slabs, _, lanes = got.shape
    width = lanes // 2
    slab_rows = X * QUAD
    copies = out.shape[0] // X
    count = slabs * slab_rows
    flat = got[:, 0:slab_rows, :].reshape(count, lanes)

    def source(lane, pairs, first):
        block = 2 * pairs * slabs
        within = lane % block
        pair = (within // slabs) % pairs + first
        return (within % slabs) * slab_rows + (lane // block) * QUAD, pair, within // (
            slabs * pairs
        )

    def turned(pairs, first):
        size = X * 2 * pairs * slabs
        lane = iota((count, size), 1)
        row = iota((count, size), 0)
        slab, pair, odd = source(lane, pairs, first)
        at = slab + pair
        even_move = jnp.where((row == at) & (odd == 0), 1.0, 0.0).astype(LOW)
        odd_move = jnp.where((row == at) & (odd == 1), 1.0, 0.0).astype(LOW)
        move = jnp.where(row == slab + (QUAD - 1), 1.0, 0.0).astype(LOW)
        data = dot(flat[:, 0:width], even_move, TN) + dot(flat[:, width:], odd_move, TN)
        spread = dot(flat, move, TN)[0:16, :]
        down = iota((16, size), 0)
        _, pair, odd = source(iota((16, size), 1), pairs, first)
        slot = 2 * (2 * pair + odd)
        high = jnp.sum(jnp.where(down == slot, spread, 0.0), axis=0, keepdims=True)
        low = jnp.sum(jnp.where(down == slot + 1, spread, 0.0), axis=0, keepdims=True)
        return data.astype(LOW), high, low

    many, many_high, many_low = turned(2, 0)
    few, few_high, few_low = turned(1, 2)
    total = jnp.sum(got[:, slab_rows:, :].astype(FULL), axis=0)
    tail = halves(total[0:4, :] + total[4:8, :])
    blank = jnp.zeros((5, lanes), FULL)
    for x in range(X):
        here = slice(x * lanes, (x + 1) * lanes)
        half = slice(x * width, (x + 1) * width)
        rest = jnp.concatenate([few[0 : width // 2, half], few[width // 2 :, half]], axis=1)
        last = jnp.concatenate(
            [
                many_high[:, here],
                many_low[:, here],
                jnp.concatenate([few_high[:, half], few_low[:, half]], axis=1),
                blank,
                tail,
            ],
            axis=0,
        ).astype(LOW)
        for j in range(copies):
            out[x * copies + j, 0:width, :] = many[:, here]
            out[x * copies + j, width : width + width // 2, :] = rest
            out[x * copies + j, width + width // 2 :, :] = last


def update_kernel(
    got,
    table,
    state,
    projection,
    projection_state,
    new_table,
    new_state,
    new_projection,
    new_projection_state,
    spread,
    marks,
    total,
    grad,
):
    reps, peers, rows, lanes = got.shape
    width, table_rows = table.shape
    half = width // 2
    low_count = marks.shape[0]
    high_count = table_rows // low_count
    marked = iota((STEP, lanes), 0).astype(FULL).astype(LOW)
    none = jnp.zeros((STEP, lanes), LOW)
    one = jnp.ones((STEP, lanes), LOW)

    def put(at, entry, high, low):
        cols = slice(at, at + lanes)
        high = jnp.broadcast_to(high, (STEP, lanes)).astype(LOW)
        low = jnp.broadcast_to(low, (STEP, lanes))
        for h in range(high_count):
            here = high == jnp.full((STEP, lanes), h, LOW)
            for r in range(0, width, STEP):
                spread[h * width + r : h * width + r + STEP, cols] = jnp.where(
                    here, entry[r : r + STEP, :], none
                )
        for r in range(0, low_count, STEP):
            marks[r : r + STEP, cols] = jnp.where(
                (low - float(r)).astype(LOW) == marked, one, none
            )

    def beside(a, b):
        first = jnp.concatenate([a[:, 0:width], b[:, 0:width]], axis=1)
        second = jnp.concatenate([a[:, width:], b[:, width:]], axis=1)
        return first, second

    at = 0
    for n in range(peers):
        pair = [got.at[r, n] for r in range(reps)]
        numbers = [block[width + half : rows, :].astype(FULL) for block in pair]
        for block, number in zip(pair, numbers, strict=True):
            put(at, block[0:width, :], number[0:1, :], number[1:2, :])
            at += lanes
        top, bottom = beside(*[block[width : width + half, :] for block in pair])
        high, low = beside(*[number[2:3, :] for number in numbers])
        put(at, jnp.concatenate([top, bottom], axis=0), high, low)
        at += lanes
    total[...] = dot(spread[...], marks[...], NT)

    for h in range(high_count):
        cols = slice(h * low_count, (h + 1) * low_count)
        dense = total[h * width : (h + 1) * width, :]
        fresh = state[:, cols] + jnp.sum(dense * dense, axis=0, keepdims=True) * (1.0 / width)
        new_state[:, cols] = fresh
        new_table[:, cols] = table[:, cols] - dense * (learn_rate / (jnp.sqrt(fresh) + epsilon))

    for i in range(reps * peers):
        r, c = 4 * (i // 2), 128 * (i % 2)
        tail = got[i % reps, i // reps, width + half : rows, :].astype(FULL)
        grad[r : r + 4, c : c + 128] = tail[8:12, :] + tail[12:16, :]
    whole = grad[...]
    fresh = projection_state[...] + whole * whole
    new_projection_state[...] = fresh
    new_projection[...] = projection[...] - learn_rate * whole / (jnp.sqrt(fresh) + epsilon)


def call(kernel, outs, *args, scratch=(), where=pltpu.VMEM, limit=40 * 2**20):
    spec = pl.BlockSpec(memory_space=pltpu.VMEM)
    return pl.pallas_call(
        kernel,
        out_shape=outs,
        in_specs=[pl.BlockSpec(memory_space=where)] * len(args),
        out_specs=jax.tree.map(lambda _: spec, outs),
        scratch_shapes=list(scratch),
        compiler_params=pltpu.CompilerParams(vmem_limit_bytes=limit),
    )(*args)


def shards(
    output_grad,
    pooled,
    bag_owners,
    bag_rows,
    bag_weights,
    embed_table,
    table_state,
    projection,
    projection_state,
):
    depth = lax.axis_size("z")
    peers = lax.axis_size(PLANE)
    reps = lax.axis_size("rep")
    table_rows, width = embed_table.shape
    lanes = 2 * width

    with jax.named_scope("route"):
        inputs = (
            output_grad,
            pooled.T,
            projection,
            bag_owners.T,
            bag_rows.T,
            bag_weights.T,
        )
        shares, sent = call(
            route_kernel,
            (
                jax.ShapeDtypeStruct((peers, 4, 128), FULL),
                jax.ShapeDtypeStruct((depth, X * QUAD, lanes), LOW),
            ),
            *inputs,
            scratch=[pltpu.VMEM(a.shape, a.dtype) for a in inputs]
            + [pltpu.SemaphoreType.DMA((len(inputs),))],
            where=pltpu.HBM,
            limit=60 * 2**20,
        )
    with jax.named_scope("weight_plane"):
        shares = lax.all_to_all(shares, PLANE, 0, 0, tiled=True)
    with jax.named_scope("join"):
        sent = call(
            join_kernel,
            jax.ShapeDtypeStruct((depth, X * QUAD + 8, lanes), LOW),
            sent,
            shares,
        )
    ring = [[(i + depth // 2) % depth for i in range(depth)]]
    with jax.named_scope("along_z"):
        got = lax.all_to_all(sent, "z", 0, 0, axis_index_groups=ring, tiled=True)
    with jax.named_scope("regroup"):
        sent = call(
            regroup_kernel,
            jax.ShapeDtypeStruct((peers // reps, width + width // 2 + 16, lanes), LOW),
            got,
        )
    with jax.named_scope("in_plane"):
        got = lax.all_to_all(sent, ("x", "col"), 0, 0, tiled=True)
    with jax.named_scope("on_chip"):
        got = lax.all_gather(got, "rep")
    with jax.named_scope("update"):
        columns = peers // 2 * 3 * lanes
        new_table, new_state, new_projection, new_projection_state = call(
            update_kernel,
            (
                jax.ShapeDtypeStruct((width, table_rows), FULL),
                jax.ShapeDtypeStruct((1, table_rows), FULL),
                jax.ShapeDtypeStruct(projection.shape, FULL),
                jax.ShapeDtypeStruct(projection.shape, FULL),
            ),
            got,
            embed_table.T,
            table_state.reshape(1, table_rows),
            projection,
            projection_state,
            scratch=(
                pltpu.VMEM((table_rows // 256 * width, columns), LOW),
                pltpu.VMEM((256, columns), LOW),
                pltpu.VMEM((table_rows // 256 * width, 256), FULL),
                pltpu.VMEM(projection.shape, FULL),
            ),
        )
    return (
        new_table.T,
        new_state.reshape(table_rows),
        new_projection,
        new_projection_state,
    )


def solution(mesh):
    sizes = mesh.shape
    fine = Mesh(
        mesh.devices.reshape(sizes["row"] // X, X, sizes["col"], sizes["rep"]),
        ("z", "x", "col", "rep"),
    )
    split = P(("z", "x", "col", "rep"), None)
    owned = ("z", "x")
    return jax.shard_map(
        shards,
        mesh=fine,
        in_specs=(split,) * 5 + (P(owned, None), P(owned), P(), P()),
        out_specs=(P(owned, None), P(owned), P(), P()),
        check_vma=False,
    )
```

```python
import functools

import jax
import jax.numpy as jnp
from jax import lax
from jax.experimental import pallas as pl
from jax.experimental.pallas import tpu as pltpu
from jax.sharding import Mesh
from jax.sharding import PartitionSpec as P

learn_rate = 0.5
epsilon = 1e-06

X = 4
Z_FIRST = 18
SHARE_FIRST = (3, 3)
ROWS_FIRST = (2, 2)
CAP = 6
STEP = 16
QUAD = 4
PLANE = ("x", "col", "rep")
LOW = jnp.bfloat16
FULL = jnp.float32

NT = (((1,), (1,)), ((), ()))
TN = (((0,), (0,)), ((), ()))


def dot(a, b, dims):
    return lax.dot_general(a, b, dims, preferred_element_type=FULL)


def iota(shape, dim):
    return lax.broadcasted_iota(jnp.int32, shape, dim)


def halves(value):
    high = value.astype(LOW).astype(FULL)
    return jnp.concatenate([high, value - high], axis=0)


def route_kernel(*refs):
    ins, outs, held, sems = refs[:6], refs[6:8], refs[8:14], refs[14]
    copies = [
        pltpu.make_async_copy(ins[n], held[n], sems.at[n]) for n in range(len(ins))
    ]
    for copy in copies:
        copy.start()
    for copy in copies:
        copy.wait()
    output_grad, pooled_t, projection, owners, rows, weights = held
    shares, out = outs

    grad = jnp.dot(pooled_t[...], output_grad[...], preferred_element_type=FULL)
    for i in range(shares.shape[0]):
        r, c = 4 * (i // 2), 128 * (i % 2)
        shares[i] = grad[r : r + 4, c : c + 128]

    bag, samples = owners.shape
    entries = bag * samples
    width = projection.shape[0]
    slabs, slab_rows, lanes = out.shape
    owner_count = slabs * X

    def flat(ref):
        return jnp.concatenate([ref[k : k + 1, :] for k in range(bag)], axis=1)

    pool_grad = dot(projection[...].astype(LOW), output_grad[...], NT)
    grads = jnp.concatenate(
        [(pool_grad * weights[k : k + 1, :]).astype(LOW) for k in range(bag)], axis=1
    )
    owner, row = flat(owners), flat(rows)
    hits = jnp.where(iota((owner_count, entries), 0) == owner, 1.0, 0.0)
    before = jnp.where(iota((entries, entries), 0) < iota((entries, entries), 1), 1.0, 0.0)
    earlier = jnp.dot(hits.astype(LOW), before.astype(LOW), preferred_element_type=FULL)
    rank = jnp.sum(hits * earlier, axis=0, keepdims=True).astype(jnp.int32)
    odd = rank & 1
    base = owner * QUAD
    pair_at = base + (rank >> 1)
    place = iota((slabs * slab_rows, entries), 0)

    def chosen(at):
        return jnp.where(place == at, 1.0, 0.0).astype(LOW)

    picks = jnp.concatenate(
        [
            chosen(jnp.where(odd == 0, pair_at, -1)),
            chosen(jnp.where(odd == 1, pair_at, -1)),
            chosen(base + (QUAD - 1)),
        ],
        axis=1,
    )
    blank = jnp.zeros((width, entries), LOW)
    lane = iota((lanes, entries), 0)
    numbers = jnp.where(lane == 2 * rank, row >> 8, 0) + jnp.where(
        lane == 2 * rank + 1, row & 255, 0
    )
    values = jnp.concatenate(
        [
            jnp.concatenate([grads, blank], axis=0),
            jnp.concatenate([blank, grads], axis=0),
            numbers.astype(FULL).astype(LOW),
        ],
        axis=1,
    )
    sent = dot(picks, values, NT).astype(LOW)
    for i in range(slabs):
        out[(i - Z_FIRST) % slabs] = sent[i * slab_rows : (i + 1) * slab_rows, :]


def join_kernel(sent, shares, out):
    slabs, slab_rows, _ = sent.shape
    share = halves(jnp.sum(shares[...], axis=0)).astype(LOW)
    for i in range(slabs):
        out[i, 0:slab_rows, :] = sent[i]
        out[i, slab_rows:, :] = share


def regroup_kernel(got, out, *, order):
    slabs, _, lanes = got.shape
    width = lanes // 2
    slab_rows = X * QUAD
    copies = len(order) // X
    count = slabs * slab_rows
    flat = got[:, 0:slab_rows, :].reshape(count, lanes)

    def source(lane, pairs, first):
        block = 2 * pairs * slabs
        within = lane % block
        pair = (within // slabs) % pairs + first
        return (within % slabs) * slab_rows + (lane // block) * QUAD, pair, within // (
            slabs * pairs
        )

    def turned(pairs, first):
        size = X * 2 * pairs * slabs
        lane = iota((count, size), 1)
        row = iota((count, size), 0)
        slab, pair, odd = source(lane, pairs, first)
        at = slab + pair
        even_move = jnp.where((row == at) & (odd == 0), 1.0, 0.0).astype(LOW)
        odd_move = jnp.where((row == at) & (odd == 1), 1.0, 0.0).astype(LOW)
        move = jnp.where(row == slab + (QUAD - 1), 1.0, 0.0).astype(LOW)
        data = dot(flat[:, 0:width], even_move, TN) + dot(flat[:, width:], odd_move, TN)
        spread = dot(flat, move, TN)[0:16, :]
        down = iota((16, size), 0)
        _, pair, odd = source(iota((16, size), 1), pairs, first)
        slot = 2 * (2 * pair + odd)
        high = jnp.sum(jnp.where(down == slot, spread, 0.0), axis=0, keepdims=True)
        low = jnp.sum(jnp.where(down == slot + 1, spread, 0.0), axis=0, keepdims=True)
        return data.astype(LOW), high, low

    many, many_high, many_low = turned(2, 0)
    few, few_high, few_low = turned(1, 2)
    total = jnp.sum(got[:, slab_rows:, :].astype(FULL), axis=0)
    tail = halves(total[0:4, :] + total[4:8, :])
    blank = jnp.zeros((5, lanes), FULL)
    for x in range(X):
        here = slice(x * lanes, (x + 1) * lanes)
        half = slice(x * width, (x + 1) * width)
        rest = jnp.concatenate([few[0 : width // 2, half], few[width // 2 :, half]], axis=1)
        last = jnp.concatenate(
            [
                many_high[:, here],
                many_low[:, here],
                jnp.concatenate([few_high[:, half], few_low[:, half]], axis=1),
                blank,
                tail,
            ],
            axis=0,
        ).astype(LOW)
        for n, device in enumerate(order):
            if device // copies == x:
                out[n, 0:width, :] = many[:, here]
                out[n, width : width + width // 2, :] = rest
                out[n, width + width // 2 :, :] = last


def update_kernel(
    got,
    table,
    state,
    projection,
    projection_state,
    new_table,
    new_state,
    new_projection,
    new_projection_state,
    spread,
    marks,
    total,
    grad,
    *,
    chunks,
):
    reps, peers, rows, lanes = got.shape
    width, table_rows = table.shape
    half = width // 2
    low_count = marks.shape[0]
    high_count = table_rows // low_count
    marked = iota((STEP, lanes), 0).astype(FULL).astype(LOW)
    none = jnp.zeros((STEP, lanes), LOW)
    one = jnp.ones((STEP, lanes), LOW)

    def put(at, entry, high, low):
        cols = slice(at, at + lanes)
        high = jnp.broadcast_to(high, (STEP, lanes)).astype(LOW)
        low = jnp.broadcast_to(low, (STEP, lanes))
        for h in range(high_count):
            here = high == jnp.full((STEP, lanes), h, LOW)
            for r in range(0, width, STEP):
                spread[h * width + r : h * width + r + STEP, cols] = jnp.where(
                    here, entry[r : r + STEP, :], none
                )
        for r in range(0, low_count, STEP):
            marks[r : r + STEP, cols] = jnp.where(
                (low - float(r)).astype(LOW) == marked, one, none
            )

    def beside(a, b):
        first = jnp.concatenate([a[:, 0:width], b[:, 0:width]], axis=1)
        second = jnp.concatenate([a[:, width:], b[:, width:]], axis=1)
        return first, second

    at = 0
    for n in range(peers):
        pair = [got.at[r, n] for r in range(reps)]
        numbers = [block[width + half : rows, :].astype(FULL) for block in pair]
        for block, number in zip(pair, numbers, strict=True):
            put(at, block[0:width, :], number[0:1, :], number[1:2, :])
            at += lanes
        top, bottom = beside(*[block[width : width + half, :] for block in pair])
        high, low = beside(*[number[2:3, :] for number in numbers])
        put(at, jnp.concatenate([top, bottom], axis=0), high, low)
        at += lanes
    total[...] = dot(spread[...], marks[...], NT)

    for h in range(high_count):
        cols = slice(h * low_count, (h + 1) * low_count)
        dense = total[h * width : (h + 1) * width, :]
        fresh = state[:, cols] + jnp.sum(dense * dense, axis=0, keepdims=True) * (1.0 / width)
        new_state[:, cols] = fresh
        new_table[:, cols] = table[:, cols] - dense * (learn_rate / (jnp.sqrt(fresh) + epsilon))

    for i in range(reps * peers):
        k = chunks[i // reps] * reps + i % reps
        r, c = 4 * (k // 2), 128 * (k % 2)
        tail = got[i % reps, i // reps, width + half : rows, :].astype(FULL)
        grad[r : r + 4, c : c + 128] = tail[8:12, :] + tail[12:16, :]
    whole = grad[...]
    fresh = projection_state[...] + whole * whole
    new_projection_state[...] = fresh
    new_projection[...] = projection[...] - learn_rate * whole / (jnp.sqrt(fresh) + epsilon)


def call(kernel, outs, *args, scratch=(), where=pltpu.VMEM, limit=40 * 2**20):
    spec = pl.BlockSpec(memory_space=pltpu.VMEM)
    return pl.pallas_call(
        kernel,
        out_shape=outs,
        in_specs=[pl.BlockSpec(memory_space=where)] * len(args),
        out_specs=jax.tree.map(lambda _: spec, outs),
        scratch_shapes=list(scratch),
        compiler_params=pltpu.CompilerParams(vmem_limit_bytes=limit),
    )(*args)


def shards(
    output_grad,
    pooled,
    bag_owners,
    bag_rows,
    bag_weights,
    embed_table,
    table_state,
    projection,
    projection_state,
):
    depth = lax.axis_size("z")
    peers = lax.axis_size(PLANE)
    reps = lax.axis_size("rep")
    table_rows, width = embed_table.shape
    lanes = 2 * width
    cols = lax.axis_size("col")

    def order(first):
        return [
            (x + first[0]) % X * cols + (c + first[1]) % cols
            for x in range(X)
            for c in range(cols)
        ]

    share_order, rows_order = order(SHARE_FIRST), order(ROWS_FIRST)
    share_group = [[d * reps + r for d in share_order for r in range(reps)]]

    with jax.named_scope("route"):
        inputs = (
            output_grad,
            pooled.T,
            projection,
            bag_owners.T,
            bag_rows.T,
            bag_weights.T,
        )
        shares, sent = call(
            route_kernel,
            (
                jax.ShapeDtypeStruct((peers, 4, 128), FULL),
                jax.ShapeDtypeStruct((depth, X * QUAD, lanes), LOW),
            ),
            *inputs,
            scratch=[pltpu.VMEM(a.shape, a.dtype) for a in inputs]
            + [pltpu.SemaphoreType.DMA((len(inputs),))],
            where=pltpu.HBM,
            limit=60 * 2**20,
        )
    with jax.named_scope("weight_plane"):
        shares = lax.all_to_all(
            shares, PLANE, 0, 0, axis_index_groups=share_group, tiled=True
        )
    with jax.named_scope("join"):
        sent = call(
            join_kernel,
            jax.ShapeDtypeStruct((depth, X * QUAD + 8, lanes), LOW),
            sent,
            shares,
        )
    ring = [[(i + Z_FIRST) % depth for i in range(depth)]]
    with jax.named_scope("along_z"):
        got = lax.all_to_all(sent, "z", 0, 0, axis_index_groups=ring, tiled=True)
    with jax.named_scope("regroup"):
        sent = call(
            functools.partial(regroup_kernel, order=rows_order),
            jax.ShapeDtypeStruct((peers // reps, width + width // 2 + 16, lanes), LOW),
            got,
        )
    with jax.named_scope("in_plane"):
        got = lax.all_to_all(
            sent, ("x", "col"), 0, 0, axis_index_groups=[rows_order], tiled=True
        )
    with jax.named_scope("on_chip"):
        got = lax.all_gather(got, "rep")
    with jax.named_scope("update"):
        columns = peers // 2 * 3 * lanes
        new_table, new_state, new_projection, new_projection_state = call(
            functools.partial(
                update_kernel, chunks=[share_order.index(d) for d in rows_order]
            ),
            (
                jax.ShapeDtypeStruct((width, table_rows), FULL),
                jax.ShapeDtypeStruct((1, table_rows), FULL),
                jax.ShapeDtypeStruct(projection.shape, FULL),
                jax.ShapeDtypeStruct(projection.shape, FULL),
            ),
            got,
            embed_table.T,
            table_state.reshape(1, table_rows),
            projection,
            projection_state,
            scratch=(
                pltpu.VMEM((table_rows // 256 * width, columns), LOW),
                pltpu.VMEM((256, columns), LOW),
                pltpu.VMEM((table_rows // 256 * width, 256), FULL),
                pltpu.VMEM(projection.shape, FULL),
            ),
        )
    return (
        new_table.T,
        new_state.reshape(table_rows),
        new_projection,
        new_projection_state,
    )


def solution(mesh):
    sizes = mesh.shape
    fine = Mesh(
        mesh.devices.reshape(sizes["row"] // X, X, sizes["col"], sizes["rep"]),
        ("z", "x", "col", "rep"),
    )
    split = P(("z", "x", "col", "rep"), None)
    owned = ("z", "x")
    return jax.shard_map(
        shards,
        mesh=fine,
        in_specs=(split,) * 5 + (P(owned, None), P(owned), P(), P()),
        out_specs=(P(owned, None), P(owned), P(), P()),
        check_vma=False,
    )
```

```python
import functools

import jax
import jax.numpy as jnp
from jax import lax
from jax.experimental import pallas as pl
from jax.experimental.pallas import tpu as pltpu
from jax.sharding import Mesh
from jax.sharding import PartitionSpec as P

learn_rate = 0.5
epsilon = 1e-06

X = 4
Z_FIRST = 18
SHARE_FIRST = (3, 3)
ROWS_FIRST = (2, 2)
CAP = 6
STEP = 16
QUAD = 4
PLANE = ("x", "col", "rep")
LOW = jnp.bfloat16
FULL = jnp.float32

NT = (((1,), (1,)), ((), ()))
TN = (((0,), (0,)), ((), ()))


def dot(a, b, dims):
    return lax.dot_general(a, b, dims, preferred_element_type=FULL)


def iota(shape, dim):
    return lax.broadcasted_iota(jnp.int32, shape, dim)


def halves(value):
    high = value.astype(LOW).astype(FULL)
    return jnp.concatenate([high, value - high], axis=0)


def fetched(ins, held, sems):
    copies = [
        pltpu.make_async_copy(ins[n], held[n], sems.at[n]) for n in range(len(ins))
    ]
    for copy in copies:
        copy.start()
    for copy in copies:
        copy.wait()
    return held


def weight_kernel(output_grad, pooled_t, shares, *held):
    output_grad, pooled_t = fetched((output_grad, pooled_t), held[:-1], held[-1])
    grad = jnp.dot(pooled_t[...], output_grad[...], preferred_element_type=FULL)
    for i in range(shares.shape[0]):
        r, c = 4 * (i // 2), 128 * (i % 2)
        shares[i] = grad[r : r + 4, c : c + 128]


def route_kernel(output_grad, projection, owners, rows, weights, out):
    bag, samples = owners.shape
    entries = bag * samples
    width = projection.shape[0]
    slabs, slab_rows, lanes = out.shape
    owner_count = slabs * X

    def flat(ref):
        return jnp.concatenate([ref[k : k + 1, :] for k in range(bag)], axis=1)

    pool_grad = dot(projection[...].astype(LOW), output_grad[...], NT)
    grads = jnp.concatenate(
        [(pool_grad * weights[k : k + 1, :]).astype(LOW) for k in range(bag)], axis=1
    )
    owner, row = flat(owners), flat(rows)
    hits = jnp.where(iota((owner_count, entries), 0) == owner, 1.0, 0.0)
    before = jnp.where(iota((entries, entries), 0) < iota((entries, entries), 1), 1.0, 0.0)
    earlier = jnp.dot(hits.astype(LOW), before.astype(LOW), preferred_element_type=FULL)
    rank = jnp.sum(hits * earlier, axis=0, keepdims=True).astype(jnp.int32)
    odd = rank & 1
    base = owner * QUAD
    pair_at = base + (rank >> 1)
    place = iota((slabs * slab_rows, entries), 0)

    def chosen(at):
        return jnp.where(place == at, 1.0, 0.0).astype(LOW)

    picks = jnp.concatenate(
        [
            chosen(jnp.where(odd == 0, pair_at, -1)),
            chosen(jnp.where(odd == 1, pair_at, -1)),
            chosen(base + (QUAD - 1)),
        ],
        axis=1,
    )
    blank = jnp.zeros((width, entries), LOW)
    lane = iota((lanes, entries), 0)
    numbers = jnp.where(lane == 2 * rank, row >> 8, 0) + jnp.where(
        lane == 2 * rank + 1, row & 255, 0
    )
    values = jnp.concatenate(
        [
            jnp.concatenate([grads, blank], axis=0),
            jnp.concatenate([blank, grads], axis=0),
            numbers.astype(FULL).astype(LOW),
        ],
        axis=1,
    )
    sent = dot(picks, values, NT).astype(LOW)
    for i in range(slabs):
        out[(i - Z_FIRST) % slabs] = sent[i * slab_rows : (i + 1) * slab_rows, :]


def join_kernel(sent, shares, out):
    slabs, slab_rows, _ = sent.shape
    share = halves(jnp.sum(shares[...], axis=0)).astype(LOW)
    for i in range(slabs):
        out[i, 0:slab_rows, :] = sent[i]
        out[i, slab_rows:, :] = share


def regroup_kernel(got, out, *, order):
    slabs, _, lanes = got.shape
    width = lanes // 2
    slab_rows = X * QUAD
    copies = len(order) // X
    count = slabs * slab_rows
    flat = got[:, 0:slab_rows, :].reshape(count, lanes)

    def source(lane, pairs, first):
        block = 2 * pairs * slabs
        within = lane % block
        pair = (within // slabs) % pairs + first
        return (within % slabs) * slab_rows + (lane // block) * QUAD, pair, within // (
            slabs * pairs
        )

    def turned(pairs, first):
        size = X * 2 * pairs * slabs
        slab, pair, odd = source(iota((1, size), 1), pairs, first)
        row = iota((count, size), 0)

        def chosen(at):
            return jnp.where(row == at, 1.0, 0.0).astype(LOW)

        even_move = chosen(jnp.where(odd == 0, slab + pair, -1))
        odd_move = chosen(jnp.where(odd == 1, slab + pair, -1))
        move = chosen(slab + (QUAD - 1))
        data = dot(flat[:, 0:width], even_move, TN) + dot(flat[:, width:], odd_move, TN)
        spread = dot(flat, move, TN)[0:16, :]
        down = iota((16, size), 0)
        slot = 2 * (2 * pair + odd)
        high = jnp.sum(jnp.where(down == slot, spread, 0.0), axis=0, keepdims=True)
        low = jnp.sum(jnp.where(down == slot + 1, spread, 0.0), axis=0, keepdims=True)
        return data.astype(LOW), high, low

    many, many_high, many_low = turned(2, 0)
    few, few_high, few_low = turned(1, 2)
    total = jnp.sum(got[:, slab_rows:, :].astype(FULL), axis=0)
    tail = halves(total[0:4, :] + total[4:8, :])
    blank = jnp.zeros((5, lanes), FULL)
    for x in range(X):
        here = slice(x * lanes, (x + 1) * lanes)
        half = slice(x * width, (x + 1) * width)
        rest = jnp.concatenate([few[0 : width // 2, half], few[width // 2 :, half]], axis=1)
        last = jnp.concatenate(
            [
                many_high[:, here],
                many_low[:, here],
                jnp.concatenate([few_high[:, half], few_low[:, half]], axis=1),
                blank,
                tail,
            ],
            axis=0,
        ).astype(LOW)
        for n, device in enumerate(order):
            if device // copies == x:
                out[n, 0:width, :] = many[:, here]
                out[n, width : width + width // 2, :] = rest
                out[n, width + width // 2 :, :] = last


def update_kernel(
    got,
    table,
    state,
    projection,
    projection_state,
    new_table,
    new_state,
    new_projection,
    new_projection_state,
    spread,
    marks,
    total,
    grad,
    *,
    chunks,
):
    reps, peers, rows, lanes = got.shape
    width, table_rows = table.shape
    half = width // 2
    low_count = marks.shape[0]
    high_count = table_rows // low_count
    marked = iota((STEP, lanes), 0).astype(FULL).astype(LOW)
    none = jnp.zeros((STEP, lanes), LOW)
    one = jnp.ones((STEP, lanes), LOW)

    def put(at, entry, high, low):
        cols = slice(at, at + lanes)
        high = jnp.broadcast_to(high, (STEP, lanes)).astype(LOW)
        low = jnp.broadcast_to(low, (STEP, lanes))
        for h in range(high_count):
            here = high == jnp.full((STEP, lanes), h, LOW)
            for r in range(0, width, STEP):
                spread[h * width + r : h * width + r + STEP, cols] = jnp.where(
                    here, entry[r : r + STEP, :], none
                )
        for r in range(0, low_count, STEP):
            marks[r : r + STEP, cols] = jnp.where(
                (low - float(r)).astype(LOW) == marked, one, none
            )

    def beside(a, b):
        first = jnp.concatenate([a[:, 0:width], b[:, 0:width]], axis=1)
        second = jnp.concatenate([a[:, width:], b[:, width:]], axis=1)
        return first, second

    at = 0
    for n in range(peers):
        pair = [got.at[r, n] for r in range(reps)]
        numbers = [block[width + half : rows, :].astype(FULL) for block in pair]
        for block, number in zip(pair, numbers, strict=True):
            put(at, block[0:width, :], number[0:1, :], number[1:2, :])
            at += lanes
        top, bottom = beside(*[block[width : width + half, :] for block in pair])
        high, low = beside(*[number[2:3, :] for number in numbers])
        put(at, jnp.concatenate([top, bottom], axis=0), high, low)
        at += lanes
    total[...] = dot(spread[...], marks[...], NT)

    for h in range(high_count):
        cols = slice(h * low_count, (h + 1) * low_count)
        dense = total[h * width : (h + 1) * width, :]
        fresh = state[:, cols] + jnp.sum(dense * dense, axis=0, keepdims=True) * (1.0 / width)
        new_state[:, cols] = fresh
        new_table[:, cols] = table[:, cols] - dense * (learn_rate / (jnp.sqrt(fresh) + epsilon))

    for i in range(reps * peers):
        k = chunks[i // reps] * reps + i % reps
        r, c = 4 * (k // 2), 128 * (k % 2)
        tail = got[i % reps, i // reps, width + half : rows, :].astype(FULL)
        grad[r : r + 4, c : c + 128] = tail[8:12, :] + tail[12:16, :]
    whole = grad[...]
    fresh = projection_state[...] + whole * whole
    new_projection_state[...] = fresh
    new_projection[...] = projection[...] - learn_rate * whole / (jnp.sqrt(fresh) + epsilon)


def call(kernel, outs, *args, scratch=(), where=pltpu.VMEM, limit=40 * 2**20):
    spec = pl.BlockSpec(memory_space=pltpu.VMEM)
    return pl.pallas_call(
        kernel,
        out_shape=outs,
        in_specs=[pl.BlockSpec(memory_space=where)] * len(args),
        out_specs=jax.tree.map(lambda _: spec, outs),
        scratch_shapes=list(scratch),
        compiler_params=pltpu.CompilerParams(vmem_limit_bytes=limit),
    )(*args)


def shards(
    output_grad,
    pooled,
    bag_owners,
    bag_rows,
    bag_weights,
    embed_table,
    table_state,
    projection,
    projection_state,
):
    depth = lax.axis_size("z")
    peers = lax.axis_size(PLANE)
    reps = lax.axis_size("rep")
    table_rows, width = embed_table.shape
    lanes = 2 * width
    cols = lax.axis_size("col")

    def order(first):
        return [
            (x + first[0]) % X * cols + (c + first[1]) % cols
            for x in range(X)
            for c in range(cols)
        ]

    share_order, rows_order = order(SHARE_FIRST), order(ROWS_FIRST)
    share_group = [[d * reps + r for d in share_order for r in range(reps)]]

    with jax.named_scope("weight"):
        inputs = (output_grad, pooled.T)
        shares = call(
            weight_kernel,
            jax.ShapeDtypeStruct((peers, 4, 128), FULL),
            *inputs,
            scratch=[pltpu.VMEM(a.shape, a.dtype) for a in inputs]
            + [pltpu.SemaphoreType.DMA((len(inputs),))],
            where=pltpu.HBM,
            limit=60 * 2**20,
        )
    with jax.named_scope("weight_plane"):
        shares = lax.all_to_all(
            shares, PLANE, 0, 0, axis_index_groups=share_group, tiled=True
        )
    with jax.named_scope("route"):
        sent = call(
            route_kernel,
            jax.ShapeDtypeStruct((depth, X * QUAD, lanes), LOW),
            output_grad,
            projection,
            bag_owners.T,
            bag_rows.T,
            bag_weights.T,
        )
    with jax.named_scope("join"):
        sent = call(
            join_kernel,
            jax.ShapeDtypeStruct((depth, X * QUAD + 8, lanes), LOW),
            sent,
            shares,
        )
    ring = [[(i + Z_FIRST) % depth for i in range(depth)]]
    with jax.named_scope("along_z"):
        got = lax.all_to_all(sent, "z", 0, 0, axis_index_groups=ring, tiled=True)
    with jax.named_scope("regroup"):
        sent = call(
            functools.partial(regroup_kernel, order=rows_order),
            jax.ShapeDtypeStruct((peers // reps, width + width // 2 + 16, lanes), LOW),
            got,
        )
    with jax.named_scope("in_plane"):
        got = lax.all_to_all(
            sent, ("x", "col"), 0, 0, axis_index_groups=[rows_order], tiled=True
        )
    with jax.named_scope("on_chip"):
        got = lax.all_gather(got, "rep")
    with jax.named_scope("update"):
        columns = peers // 2 * 3 * lanes
        new_table, new_state, new_projection, new_projection_state = call(
            functools.partial(
                update_kernel, chunks=[share_order.index(d) for d in rows_order]
            ),
            (
                jax.ShapeDtypeStruct((width, table_rows), FULL),
                jax.ShapeDtypeStruct((1, table_rows), FULL),
                jax.ShapeDtypeStruct(projection.shape, FULL),
                jax.ShapeDtypeStruct(projection.shape, FULL),
            ),
            got,
            embed_table.T,
            table_state.reshape(1, table_rows),
            projection,
            projection_state,
            scratch=(
                pltpu.VMEM((table_rows // 256 * width, columns), LOW),
                pltpu.VMEM((256, columns), LOW),
                pltpu.VMEM((table_rows // 256 * width, 256), FULL),
                pltpu.VMEM(projection.shape, FULL),
            ),
        )
    return (
        new_table.T,
        new_state.reshape(table_rows),
        new_projection,
        new_projection_state,
    )


def solution(mesh):
    sizes = mesh.shape
    fine = Mesh(
        mesh.devices.reshape(sizes["row"] // X, X, sizes["col"], sizes["rep"]),
        ("z", "x", "col", "rep"),
    )
    split = P(("z", "x", "col", "rep"), None)
    owned = ("z", "x")
    return jax.shard_map(
        shards,
        mesh=fine,
        in_specs=(split,) * 5 + (P(owned, None), P(owned), P(), P()),
        out_specs=(P(owned, None), P(owned), P(), P()),
        check_vma=False,
    )
```

```python
import functools

import jax
import jax.numpy as jnp
from jax import lax
from jax.experimental import pallas as pl
from jax.experimental.pallas import tpu as pltpu
from jax.sharding import Mesh
from jax.sharding import PartitionSpec as P

learn_rate = 0.5
epsilon = 1e-06

X = 4
Z_FIRST = 20
SHARE_FIRST = (3, 3)
ROWS_FIRST = (2, 2)
CAP = 6
STEP = 16
QUAD = 4
PLANE = ("x", "col", "rep")
LOW = jnp.bfloat16
FULL = jnp.float32

NT = (((1,), (1,)), ((), ()))
TN = (((0,), (0,)), ((), ()))


def dot(a, b, dims):
    return lax.dot_general(a, b, dims, preferred_element_type=FULL)


def iota(shape, dim):
    return lax.broadcasted_iota(jnp.int32, shape, dim)


def halves(value):
    high = value.astype(LOW).astype(FULL)
    return jnp.concatenate([high, value - high], axis=0)


def fetched(ins, held, sems):
    copies = [
        pltpu.make_async_copy(ins[n], held[n], sems.at[n]) for n in range(len(ins))
    ]
    for copy in copies:
        copy.start()
    for copy in copies:
        copy.wait()
    return held


def weight_kernel(output_grad, pooled_t, shares, *held):
    output_grad, pooled_t = fetched((output_grad, pooled_t), held[:-1], held[-1])
    grad = jnp.dot(pooled_t[...], output_grad[...], preferred_element_type=FULL)
    for i in range(shares.shape[0]):
        r, c = 4 * (i // 2), 128 * (i % 2)
        shares[i] = grad[r : r + 4, c : c + 128]


def route_kernel(output_grad, projection, owners, rows, weights, out):
    bag, samples = owners.shape
    entries = bag * samples
    width = projection.shape[0]
    slabs, slab_rows, lanes = out.shape
    owner_count = slabs * X

    def flat(ref):
        return jnp.concatenate([ref[k : k + 1, :] for k in range(bag)], axis=1)

    pool_grad = dot(projection[...].astype(LOW), output_grad[...], NT)
    grads = jnp.concatenate(
        [(pool_grad * weights[k : k + 1, :]).astype(LOW) for k in range(bag)], axis=1
    )
    owner, row = flat(owners), flat(rows)
    hits = jnp.where(iota((owner_count, entries), 0) == owner, 1.0, 0.0)
    before = jnp.where(iota((entries, entries), 0) < iota((entries, entries), 1), 1.0, 0.0)
    earlier = jnp.dot(hits.astype(LOW), before.astype(LOW), preferred_element_type=FULL)
    rank = jnp.sum(hits * earlier, axis=0, keepdims=True).astype(jnp.int32)
    odd = rank & 1
    base = owner * QUAD
    pair_at = base + (rank >> 1)
    place = iota((slabs * slab_rows, entries), 0)

    def chosen(at):
        return jnp.where(place == at, 1.0, 0.0).astype(LOW)

    picks = jnp.concatenate(
        [
            chosen(jnp.where(odd == 0, pair_at, -1)),
            chosen(jnp.where(odd == 1, pair_at, -1)),
            chosen(base + (QUAD - 1)),
        ],
        axis=1,
    )
    blank = jnp.zeros((width, entries), LOW)
    lane = iota((lanes, entries), 0)
    numbers = jnp.where(lane == 2 * rank, row >> 8, 0) + jnp.where(
        lane == 2 * rank + 1, row & 255, 0
    )
    values = jnp.concatenate(
        [
            jnp.concatenate([grads, blank], axis=0),
            jnp.concatenate([blank, grads], axis=0),
            numbers.astype(FULL).astype(LOW),
        ],
        axis=1,
    )
    sent = dot(picks, values, NT).astype(LOW)
    for i in range(slabs):
        out[(i - Z_FIRST) % slabs] = sent[i * slab_rows : (i + 1) * slab_rows, :]


def join_kernel(sent, shares, out):
    slabs, slab_rows, _ = sent.shape
    share = halves(jnp.sum(shares[...], axis=0)).astype(LOW)
    for i in range(slabs):
        out[i, 0:slab_rows, :] = sent[i]
        out[i, slab_rows:, :] = share


def regroup_kernel(got, out, *, order):
    slabs, _, lanes = got.shape
    width = lanes // 2
    slab_rows = X * QUAD
    copies = len(order) // X
    count = slabs * slab_rows
    flat = got[:, 0:slab_rows, :].reshape(count, lanes)

    def source(lane, pairs, first):
        block = 2 * pairs * slabs
        within = lane % block
        pair = (within // slabs) % pairs + first
        return (within % slabs) * slab_rows + (lane // block) * QUAD, pair, within // (
            slabs * pairs
        )

    def turned(pairs, first):
        size = X * 2 * pairs * slabs
        slab, pair, odd = source(iota((1, size), 1), pairs, first)
        row = iota((count, size), 0)

        def chosen(at):
            return jnp.where(row == at, 1.0, 0.0).astype(LOW)

        even_move = chosen(jnp.where(odd == 0, slab + pair, -1))
        odd_move = chosen(jnp.where(odd == 1, slab + pair, -1))
        move = chosen(slab + (QUAD - 1))
        data = dot(flat[:, 0:width], even_move, TN) + dot(flat[:, width:], odd_move, TN)
        spread = dot(flat, move, TN)[0:16, :]
        down = iota((16, size), 0)
        slot = 2 * (2 * pair + odd)
        high = jnp.sum(jnp.where(down == slot, spread, 0.0), axis=0, keepdims=True)
        low = jnp.sum(jnp.where(down == slot + 1, spread, 0.0), axis=0, keepdims=True)
        return data.astype(LOW), high, low

    many, many_high, many_low = turned(2, 0)
    few, few_high, few_low = turned(1, 2)
    total = jnp.sum(got[:, slab_rows:, :].astype(FULL), axis=0)
    tail = halves(total[0:4, :] + total[4:8, :])
    blank = jnp.zeros((5, lanes), FULL)
    for x in range(X):
        here = slice(x * lanes, (x + 1) * lanes)
        half = slice(x * width, (x + 1) * width)
        rest = jnp.concatenate([few[0 : width // 2, half], few[width // 2 :, half]], axis=1)
        last = jnp.concatenate(
            [
                many_high[:, here],
                many_low[:, here],
                jnp.concatenate([few_high[:, half], few_low[:, half]], axis=1),
                blank,
                tail,
            ],
            axis=0,
        ).astype(LOW)
        for n, device in enumerate(order):
            if device // copies == x:
                out[n, 0:width, :] = many[:, here]
                out[n, width : width + width // 2, :] = rest
                out[n, width + width // 2 :, :] = last


def update_kernel(
    got,
    table,
    state,
    projection,
    projection_state,
    new_table,
    new_state,
    new_projection,
    new_projection_state,
    spread,
    marks,
    total,
    grad,
    *,
    chunks,
):
    reps, peers, rows, lanes = got.shape
    width, table_rows = table.shape
    half = width // 2
    low_count = marks.shape[0]
    high_count = table_rows // low_count
    marked = iota((STEP, lanes), 0).astype(FULL).astype(LOW)
    none = jnp.zeros((STEP, lanes), LOW)
    one = jnp.ones((STEP, lanes), LOW)

    def put(at, entry, high, low):
        cols = slice(at, at + lanes)
        high = jnp.broadcast_to(high, (STEP, lanes)).astype(LOW)
        low = jnp.broadcast_to(low, (STEP, lanes))
        for h in range(high_count):
            here = high == jnp.full((STEP, lanes), h, LOW)
            for r in range(0, width, STEP):
                spread[h * width + r : h * width + r + STEP, cols] = jnp.where(
                    here, entry[r : r + STEP, :], none
                )
        for r in range(0, low_count, STEP):
            marks[r : r + STEP, cols] = jnp.where(
                (low - float(r)).astype(LOW) == marked, one, none
            )

    def beside(a, b):
        first = jnp.concatenate([a[:, 0:width], b[:, 0:width]], axis=1)
        second = jnp.concatenate([a[:, width:], b[:, width:]], axis=1)
        return first, second

    at = 0
    for n in range(peers):
        pair = [got.at[r, n] for r in range(reps)]
        numbers = [block[width + half : rows, :].astype(FULL) for block in pair]
        for block, number in zip(pair, numbers, strict=True):
            put(at, block[0:width, :], number[0:1, :], number[1:2, :])
            at += lanes
        top, bottom = beside(*[block[width : width + half, :] for block in pair])
        high, low = beside(*[number[2:3, :] for number in numbers])
        put(at, jnp.concatenate([top, bottom], axis=0), high, low)
        at += lanes
    total[...] = dot(spread[...], marks[...], NT)

    for h in range(high_count):
        cols = slice(h * low_count, (h + 1) * low_count)
        dense = total[h * width : (h + 1) * width, :]
        fresh = state[:, cols] + jnp.sum(dense * dense, axis=0, keepdims=True) * (1.0 / width)
        new_state[:, cols] = fresh
        new_table[:, cols] = table[:, cols] - dense * (learn_rate / (jnp.sqrt(fresh) + epsilon))

    for i in range(reps * peers):
        k = chunks[i // reps] * reps + i % reps
        r, c = 4 * (k // 2), 128 * (k % 2)
        tail = got[i % reps, i // reps, width + half : rows, :].astype(FULL)
        grad[r : r + 4, c : c + 128] = tail[8:12, :] + tail[12:16, :]
    whole = grad[...]
    fresh = projection_state[...] + whole * whole
    new_projection_state[...] = fresh
    new_projection[...] = projection[...] - learn_rate * whole / (jnp.sqrt(fresh) + epsilon)


def call(kernel, outs, *args, scratch=(), where=pltpu.VMEM, limit=40 * 2**20):
    spec = pl.BlockSpec(memory_space=pltpu.VMEM)
    return pl.pallas_call(
        kernel,
        out_shape=outs,
        in_specs=[pl.BlockSpec(memory_space=where)] * len(args),
        out_specs=jax.tree.map(lambda _: spec, outs),
        scratch_shapes=list(scratch),
        compiler_params=pltpu.CompilerParams(vmem_limit_bytes=limit),
    )(*args)


def shards(
    output_grad,
    pooled,
    bag_owners,
    bag_rows,
    bag_weights,
    embed_table,
    table_state,
    projection,
    projection_state,
):
    depth = lax.axis_size("z")
    peers = lax.axis_size(PLANE)
    reps = lax.axis_size("rep")
    table_rows, width = embed_table.shape
    lanes = 2 * width
    cols = lax.axis_size("col")

    def order(first):
        return [
            (x + first[0]) % X * cols + (c + first[1]) % cols
            for x in range(X)
            for c in range(cols)
        ]

    share_order, rows_order = order(SHARE_FIRST), order(ROWS_FIRST)
    share_group = [[d * reps + r for d in share_order for r in range(reps)]]

    with jax.named_scope("weight"):
        inputs = (output_grad, pooled.T)
        shares = call(
            weight_kernel,
            jax.ShapeDtypeStruct((peers, 4, 128), FULL),
            *inputs,
            scratch=[pltpu.VMEM(a.shape, a.dtype) for a in inputs]
            + [pltpu.SemaphoreType.DMA((len(inputs),))],
            where=pltpu.HBM,
            limit=60 * 2**20,
        )
    with jax.named_scope("weight_plane"):
        shares = lax.all_to_all(
            shares, PLANE, 0, 0, axis_index_groups=share_group, tiled=True
        )
    with jax.named_scope("route"):
        sent = call(
            route_kernel,
            jax.ShapeDtypeStruct((depth, X * QUAD, lanes), LOW),
            output_grad,
            projection,
            bag_owners.T,
            bag_rows.T,
            bag_weights.T,
        )
    with jax.named_scope("join"):
        sent = call(
            join_kernel,
            jax.ShapeDtypeStruct((depth, X * QUAD + 8, lanes), LOW),
            sent,
            shares,
        )
    ring = [[(i + Z_FIRST) % depth for i in range(depth)]]
    with jax.named_scope("along_z"):
        got = lax.all_to_all(sent, "z", 0, 0, axis_index_groups=ring, tiled=True)
    with jax.named_scope("regroup"):
        sent = call(
            functools.partial(regroup_kernel, order=rows_order),
            jax.ShapeDtypeStruct((peers // reps, width + width // 2 + 16, lanes), LOW),
            got,
        )
    with jax.named_scope("in_plane"):
        got = lax.all_to_all(
            sent, ("x", "col"), 0, 0, axis_index_groups=[rows_order], tiled=True
        )
    with jax.named_scope("on_chip"):
        got = lax.all_gather(got, "rep")
    with jax.named_scope("update"):
        columns = peers // 2 * 3 * lanes
        new_table, new_state, new_projection, new_projection_state = call(
            functools.partial(
                update_kernel, chunks=[share_order.index(d) for d in rows_order]
            ),
            (
                jax.ShapeDtypeStruct((width, table_rows), FULL),
                jax.ShapeDtypeStruct((1, table_rows), FULL),
                jax.ShapeDtypeStruct(projection.shape, FULL),
                jax.ShapeDtypeStruct(projection.shape, FULL),
            ),
            got,
            embed_table.T,
            table_state.reshape(1, table_rows),
            projection,
            projection_state,
            scratch=(
                pltpu.VMEM((table_rows // 256 * width, columns), LOW),
                pltpu.VMEM((256, columns), LOW),
                pltpu.VMEM((table_rows // 256 * width, 256), FULL),
                pltpu.VMEM(projection.shape, FULL),
            ),
        )
    return (
        new_table.T,
        new_state.reshape(table_rows),
        new_projection,
        new_projection_state,
    )


def solution(mesh):
    sizes = mesh.shape
    fine = Mesh(
        mesh.devices.reshape(sizes["row"] // X, X, sizes["col"], sizes["rep"]),
        ("z", "x", "col", "rep"),
    )
    split = P(("z", "x", "col", "rep"), None)
    owned = ("z", "x")
    return jax.shard_map(
        shards,
        mesh=fine,
        in_specs=(split,) * 5 + (P(owned, None), P(owned), P(), P()),
        out_specs=(P(owned, None), P(owned), P(), P()),
        check_vma=False,
    )
```
